128 devices in a mesh: dp: 16 (over x, y), tensor: 8 (over z, core).
Axes of the slice: x: 4, y: 4, z: 4, core: 2. Of those that a mesh axis runs over, the one named last changes fastest.
Arguments:
- grad_partial: bfloat16 [8, 32, 1024, 1024], P('tensor', None, 'dp'), may hold values from -0.0625 to 0.0625
- slot_of_block: int32 [32], replicated, may hold values from 0 to 63, as said below
- left_factor: float32 [64, 1024, 1024], P('dp', 'tensor'), as said below
- right_factor: float32 [64, 1024, 1024], P('dp', 'tensor'), as said below
- left_basis: bfloat16 [64, 1024, 1024], P('dp', 'tensor'), may hold values from -0.1875 to 0.1875
- right_basis: bfloat16 [64, 1024, 1024], P('dp', None, 'tensor'), may hold values from -0.1875 to 0.1875
- first_moment: float32 [64, 1024, 1024], P('dp', None, 'tensor'), may hold values from -0.1875 to 0.1875
- second_moment: float32 [64, 1024, 1024], P('dp', None, 'tensor'), as said below
Outputs:
- update: bfloat16 [32, 1024, 1024], P(None, 'dp', 'tensor')
- new_left: float32 [64, 1024, 1024], P('dp', 'tensor')
- new_right: float32 [64, 1024, 1024], P('dp', 'tensor')
- new_first: float32 [64, 1024, 1024], P('dp', None, 'tensor')
- new_second: float32 [64, 1024, 1024], P('dp', None, 'tensor')
The draws below stay inside these ranges and needn't reach their ends.
Inputs may be any that keep to these rules, and one draw needn't show every extreme that they name: All entries differ; the owner of block b is slot_of_block[b] // 4; some owner holds exactly 4 blocks. `left_factor`: symmetric. `right_factor`: symmetric. `second_moment`: positive.
All inputs are finite; a program needn't handle non-finite values.
Results may differ from the reference program's by a relative error of at most 0.022.
Values may be sent and summed in bfloat16 or wider, within the bound.
A program may use at most 128 MiB of HBM per device.

```python
import math
import jax
import jax.numpy as jnp
from jax import lax

B = 1024
CAP = 4
NBLK = 32
SLOTS = 64
N_DP = 16
N_TENSOR = 8


def draw_slot_of_block(key, part):
    key = jax.random.fold_in(key, 11)
    key_full, key_perm, key_shuffle = jax.random.split(key, 3)
    full_owner = jax.random.randint(key_full, (), 0, SLOTS // CAP).astype(jnp.int32)
    perm = jax.random.permutation(key_perm, SLOTS).astype(jnp.int32)
    inside = (perm // CAP == full_owner).astype(jnp.int32)
    order = jnp.argsort(inside, stable=True)
    others = perm[order][:NBLK - CAP]
    chosen = jnp.concatenate([full_owner * CAP + jnp.arange(CAP, dtype=jnp.int32), others])
    shuffle = jax.random.permutation(key_shuffle, NBLK)
    return chosen[shuffle].astype(jnp.int32)


def build_factor(key, noise):
    diagonal = jnp.exp(jax.random.uniform(key, (SLOTS, B), minval=math.log(0.5), maxval=math.log(2.0)))
    symmetric = (noise + jnp.swapaxes(noise, 1, 2)) * (0.5 / math.sqrt(2.0 * B))
    identity = (jnp.arange(B)[:, None] == jnp.arange(B)[None, :]).astype(jnp.float32)
    return symmetric + identity[None, :, :] * diagonal[:, :, None]


def draw_left_factor(key, part):
    key = jax.random.fold_in(key, 21)
    key_diag, key_noise = jax.random.split(key)
    noise = jax.random.normal(key_noise, (SLOTS, B, B))
    return build_factor(key_diag, noise)


def draw_right_factor(key, part):
    key = jax.random.fold_in(key, 31)
    key_diag, key_noise = jax.random.split(key)
    noise = jax.random.normal(key_noise, (SLOTS, B, B))
    return build_factor(key_diag, noise)


def draw_second_moment(key, part):
    key = jax.random.fold_in(key, 41)
    values = jnp.exp(jax.random.uniform(key, (SLOTS, B, B), minval=math.log(0.1), maxval=math.log(10.0)))
    return values / B


def shard_levels(key, shape, shards, least, top_value):
    def one(dim, shards_of):
        heights = jax.random.uniform(jax.random.fold_in(jax.random.fold_in(key, 6), dim), (shards_of,), jnp.float32, least / len(shards), top_value / len(shards))
        return jnp.repeat(jnp.exp(heights), shape[dim] // shards_of).reshape((-1,) + (1,) * (len(shape) - dim - 1))

    level = one(*shards[0])
    for cut in shards[1:]:
        level = level * one(*cut)
    return level


def scatter_about(stream_key, dims, scale, most, cuts=(), kind=jnp.bfloat16):
    level = shard_levels(stream_key, dims, cuts, -0.22, 0.18) if cuts else 1.0
    entries = jax.random.normal(stream_key, dims, jnp.float32) * scale * level
    return jnp.minimum(jnp.maximum(entries, -most), most).astype(kind)


def setup_inputs(seed: int = 0) -> dict:
    keys = jax.random.split(jax.random.key(seed), 9)
    grad_partial = scatter_about(keys[0], (N_TENSOR, NBLK, B, B), (B * N_TENSOR) ** -0.5, 0.0625, ((0, 8), (2, 16)))
    slot_of_block = draw_slot_of_block(jax.random.fold_in(keys[8], 71), 0)
    left_factor = draw_left_factor(jax.random.fold_in(keys[8], 71), 0)
    right_factor = draw_right_factor(jax.random.fold_in(keys[8], 71), 0)
    left_basis = scatter_about(keys[4], (SLOTS, B, B), B ** -0.5, 0.1875, ((0, 16), (1, 8)))
    right_basis = scatter_about(keys[5], (SLOTS, B, B), B ** -0.5, 0.1875, ((0, 16), (2, 8)))
    first_moment = scatter_about(keys[6], (SLOTS, B, B), B ** -0.5, 0.1875, ((0, 16), (2, 8)), jnp.float32)
    second_moment = draw_second_moment(jax.random.fold_in(keys[8], 71), 0)
    return {"grad_partial": grad_partial, "slot_of_block": slot_of_block, "left_factor": left_factor, "right_factor": right_factor, "left_basis": left_basis, "right_basis": right_basis, "first_moment": first_moment, "second_moment": second_moment}


first_beta = 0.9
second_beta = 0.95
epsilon = 1e-08

def precondition(items):
    gradient, left_old, right_old, left_rot, right_rot, first_old, second_old = items
    outer_left = jnp.dot(gradient, gradient.T, preferred_element_type=jnp.float32)
    outer_right = jnp.dot(gradient.T, gradient, preferred_element_type=jnp.float32)
    left_new = second_beta * left_old + (1.0 - second_beta) * outer_left
    right_new = second_beta * right_old + (1.0 - second_beta) * outer_right
    rotated = jnp.dot(gradient, right_rot, preferred_element_type=jnp.float32).astype(jnp.bfloat16)
    eigen_grad = jnp.dot(left_rot, rotated, preferred_element_type=jnp.float32)
    first_new = first_beta * first_old + (1.0 - first_beta) * eigen_grad
    second_new = second_beta * second_old + (1.0 - second_beta) * eigen_grad * eigen_grad
    normed = (first_new / (jnp.sqrt(second_new) + epsilon)).astype(jnp.bfloat16)
    back = jnp.dot(left_rot.T, normed, preferred_element_type=jnp.float32).astype(jnp.bfloat16)
    slab_width = B // N_TENSOR
    back_parts = back.reshape(B, N_TENSOR, slab_width).astype(jnp.float32)
    basis_parts = right_rot.reshape(B, N_TENSOR, slab_width).astype(jnp.float32)
    terms = jnp.einsum('atr,btr->tab', back_parts, basis_parts)
    rounded = lax.optimization_barrier(terms.astype(jnp.bfloat16))
    block_update = lax.optimization_barrier(jnp.sum(rounded.astype(jnp.float32), axis=0)).astype(jnp.bfloat16)
    return (block_update, left_new, right_new, first_new, second_new)

def reference(grad_partial, slot_of_block, left_factor, right_factor, left_basis, right_basis, first_moment, second_moment):
    gradient = lax.optimization_barrier(jnp.sum(grad_partial.astype(jnp.float32), axis=0)).astype(jnp.bfloat16)
    slotted = jnp.zeros((CAP * N_DP, B, B), gradient.dtype).at[slot_of_block].set(gradient)
    updates, new_left, new_right, new_first, new_second = lax.map(precondition, (slotted, left_factor, right_factor, left_basis, right_basis, first_moment, second_moment))
    update = updates[slot_of_block]
    return (update, new_left, new_right, new_first, new_second)
```

```python
import jax
import jax.numpy as jnp
from jax import lax
from jax.sharding import PartitionSpec as P

first_beta = 0.9
second_beta = 0.95
epsilon = 1e-08


def per_device(
    grad_partial,
    slot_of_block,
    left_factor,
    right_factor,
    left_basis,
    right_basis,
    first_moment,
    second_moment,
):
    local_part = grad_partial[0]
    block_count = local_part.shape[0]
    dp_rows = local_part.shape[1]
    owned_slots = left_factor.shape[0]
    slab_width = left_factor.shape[1]
    owner_count = lax.axis_size("dp")
    slot_ids = jnp.arange(owner_count * owned_slots, dtype=jnp.int32)
    take_slot = (slot_of_block[:, None] == slot_ids[None, :]).astype(jnp.bfloat16)
    summed = lax.psum_scatter(local_part, "tensor", scatter_dimension=2, tiled=True)
    outgoing = jnp.einsum(
        "bs,brc->src", take_slot, summed, preferred_element_type=jnp.float32
    ).astype(jnp.bfloat16)
    outgoing = outgoing.reshape(owner_count, owned_slots, dp_rows, slab_width)
    incoming = lax.all_to_all(outgoing, "dp", split_axis=0, concat_axis=0, tiled=True)
    grad_slots = incoming.transpose(1, 0, 2, 3).reshape(
        owned_slots, owner_count * dp_rows, slab_width
    )
    full_grad, full_left = (
        lax.all_gather(grad_slots, "tensor", axis=2, tiled=True),
        lax.all_gather(left_basis, "tensor", axis=1, tiled=True),
    )
    row_start = lax.axis_index("tensor") * slab_width
    grad_band = lax.dynamic_slice_in_dim(full_grad, row_start, slab_width, 1)
    outer_left = jnp.einsum(
        "jrk,jck->jrc", grad_band, full_grad, preferred_element_type=jnp.float32
    )
    outer_right = jnp.einsum(
        "jkr,jkc->jrc", grad_slots, full_grad, preferred_element_type=jnp.float32
    )
    new_left = second_beta * left_factor + (1.0 - second_beta) * outer_left
    new_right = second_beta * right_factor + (1.0 - second_beta) * outer_right
    rotated = jnp.einsum(
        "jak,jkr->jar", full_grad, right_basis, preferred_element_type=jnp.float32
    ).astype(jnp.bfloat16)
    eigen_grad = jnp.einsum("jak,jkr->jar", full_left, rotated, preferred_element_type=jnp.float32)
    new_first = first_beta * first_moment + (1.0 - first_beta) * eigen_grad
    new_second = second_beta * second_moment + (1.0 - second_beta) * eigen_grad * eigen_grad
    normed = (new_first / (jnp.sqrt(new_second) + epsilon)).astype(jnp.bfloat16)
    back = jnp.einsum("jka,jkr->jar", full_left, normed, preferred_element_type=jnp.float32).astype(
        jnp.bfloat16
    )
    update_cols = lax.psum_scatter(
        jnp.einsum("jar,jcr->cja", back, right_basis, preferred_element_type=jnp.float32).astype(
            jnp.bfloat16
        ),
        "tensor",
        scatter_dimension=0,
        tiled=True,
    )
    returned = lax.all_to_all(update_cols, "dp", split_axis=2, concat_axis=1, tiled=True)
    update = jnp.einsum(
        "bs,ksr->brk", take_slot, returned, preferred_element_type=jnp.float32
    ).astype(jnp.bfloat16)
    return (update, new_left, new_right, new_first, new_second)


def solution(mesh):
    in_specs = (
        P("tensor", None, "dp", None),
        P(),
        P("dp", "tensor", None),
        P("dp", "tensor", None),
        P("dp", "tensor", None),
        P("dp", None, "tensor"),
        P("dp", None, "tensor"),
        P("dp", None, "tensor"),
    )
    out_specs = (
        P(None, "dp", "tensor"),
        P("dp", "tensor", None),
        P("dp", "tensor", None),
        P("dp", None, "tensor"),
        P("dp", None, "tensor"),
    )
    return jax.shard_map(
        per_device, mesh=mesh, in_specs=in_specs, out_specs=out_specs, check_vma=False
    )
```

```python
import functools
import jax
import jax.numpy as jnp
from jax import lax
from jax.experimental import pallas as pl
from jax.experimental.pallas import tpu as pltpu
from jax.sharding import PartitionSpec as P

first_beta = 0.9
second_beta = 0.95
epsilon = 1e-08
f32 = jnp.float32
bf16 = jnp.bfloat16
CHUNKS = 4


def aligned(index, size):
    return pl.ds(pl.multiple_of(index * size, size), size)


def dot(a, b, dims):
    return lax.dot_general(a, b, (dims, ((), ())), preferred_element_type=f32)


def step_kernel(
    n_dp,
    nz,
    slot_ref,
    inv_ref,
    gp,
    lb,
    rb,
    first_hbm,
    second_hbm,
    upd,
    ein,
    ggt_in,
    gtg_in,
    mine,
    sibr,
    rsr,
    summed,
    stage,
    grad,
    left,
    right,
    rot,
    eig,
    first,
    second,
    nout,
    normed,
    back,
    ggo,
    gto,
    ucols,
    uin,
    load_sem,
    mine_sem,
    sib_ss,
    sib_rs,
    rs_ss,
    rs_rs,
    a_ss,
    a_rs,
    r_ss,
    r_rs,
    l_ss,
    l_rs,
    gg_ss,
    gg_rs,
    gt_ss,
    gt_rs,
    e_ss,
    e_rs,
    n_ss,
    n_rs,
    g_sib_ss,
    g_sib_rs,
    l_sib_ss,
    l_sib_rs,
    b_sib_ss,
    b_sib_rs,
    one_ss,
    one_rs,
):
    blocks, rows, order = gp.shape
    width = lb.shape[1]
    size = order // CHUNKS
    dp = lax.axis_index("dp")
    t = lax.axis_index("tensor")
    z = t // 2
    c = t % 2
    sibling = (dp, 2 * z + 1 - c)
    devices = n_dp * nz

    def peer(o, k):
        return (o, 2 * k + c)

    def send(src, dst, ss, rs, dev):
        copy = pltpu.make_async_remote_copy(
            src_ref=src,
            dst_ref=dst,
            send_sem=ss,
            recv_sem=rs,
            device_id=dev,
            device_id_type=pl.DeviceIdType.MESH,
        )
        copy.start()
        return copy

    def local(src, dst, sem):
        copy = pltpu.make_async_copy(src, dst, sem)
        copy.start()
        return copy

    def plus(i):
        return lax.rem(z + i, nz)

    def minus(i):
        return lax.rem(z + nz - i, nz)

    def partner(i):
        return lax.rem(dp + i // nz, n_dp), lax.rem(z + i % nz, nz)

    load_first = local(first_hbm, first, load_sem.at[0])
    load_second = local(second_hbm, second, load_sem.at[1])
    turns = [i for i in range(1, nz)] + [0]
    mine_copies = {}
    for i in turns:
        mine_copies[i] = local(
            gp.at[:, :, aligned(2 * plus(i) + c, width)], mine.at[i], mine_sem.at[i]
        )

    barrier = pltpu.get_barrier_semaphore()

    @pl.loop(1, devices)
    def _(i):
        o, k = partner(i)
        pl.semaphore_signal(
            barrier, inc=1, device_id=peer(o, k), device_id_type=pl.DeviceIdType.MESH
        )

    pl.semaphore_signal(
        barrier, inc=1, device_id=sibling, device_id_type=pl.DeviceIdType.MESH
    )
    pl.semaphore_wait(barrier, devices)

    sib_copies = {}
    for i in turns:
        sib_copies[i] = send(
            gp.at[:, :, aligned(2 * plus(i) + 1 - c, width)],
            sibr.at[i],
            sib_ss.at[i],
            sib_rs.at[i],
            sibling,
        )

    r_copies = [
        send(
            rb.at[plus(i)],
            right.at[c, :, aligned(z, width)],
            r_ss.at[i],
            r_rs.at[i],
            peer(dp, plus(i)),
        )
        for i in range(1, nz)
    ]
    r_own = local(rb.at[z], right.at[c, :, aligned(z, width)], r_rs.at[0])

    step = 4
    rs_copies = []
    for i in turns:
        mine_copies[i].wait()
        sib_copies[i].wait_recv()
        if i:

            @pl.loop(0, blocks // step)
            def _(b):
                at = pl.ds(b * step, step)
                mine[i, at] = (mine[i, at].astype(f32) + sibr[i, at].astype(f32)).astype(bf16)

            rs_copies.append(
                send(mine.at[i], rsr.at[i], rs_ss.at[i], rs_rs.at[i], peer(dp, plus(i)))
            )
    for copy in rs_copies:
        copy.wait_recv()

    @pl.loop(0, blocks // step)
    def _(b):
        at = pl.ds(b * step, step)
        total = mine[0, at].astype(f32) + sibr[0, at].astype(f32)
        for i in range(1, nz):
            total = total + rsr[i, at].astype(f32)
        summed[at] = total.astype(bf16)

    summed[blocks] = jnp.zeros((rows, width), bf16)

    band_rows = aligned(dp, rows)
    band_cols = aligned(2 * z + c, width)

    def slot_rows(i):
        o, k = partner(i)
        s = o * nz + k
        stage[i] = summed[inv_ref[s]]
        return o, k

    @pl.loop(1, devices)
    def _(i):
        o, k = slot_rows(i)
        send(stage.at[i], grad.at[band_rows, band_cols], a_ss.at[0], a_rs.at[0], peer(o, k))

    slot_rows(0)
    local(stage.at[0], grad.at[band_rows, band_cols], a_rs.at[0])

    l_copies = [
        send(
            lb.at[plus(i)],
            left.at[aligned(2 * z + c, width)],
            l_ss.at[i],
            l_rs.at[i],
            peer(dp, plus(i)),
        )
        for i in range(1, nz)
    ]
    l_own = local(lb.at[z], left.at[aligned(2 * z + c, width)], l_rs.at[0])

    r_own.wait()
    for copy in r_copies:
        copy.wait_recv()
    r_sib = send(right.at[c], right.at[c], one_ss.at[0], one_rs.at[0], sibling)
    l_own.wait()
    for copy in l_copies:
        copy.wait_recv()
    l_sib = []
    for j in range(nz):
        band = left.at[aligned(2 * j + c, width)]
        l_sib.append(send(band, band, l_sib_ss.at[j], l_sib_rs.at[j], sibling))

    half = grad.at[:, pl.ds(0, nz * width)]
    pltpu.make_async_copy(half, half, a_rs.at[0]).wait()
    g_sib = []
    for j in range(nz):
        band = grad.at[:, aligned(2 * j + c, width)]
        g_sib.append(send(band, band, g_sib_ss.at[j], g_sib_rs.at[j], sibling))
    for copy in g_sib:
        copy.wait_recv()

    @pl.loop(0, CHUNKS)
    def _(r):
        at = aligned(r, size)
        rot[at] = dot(grad[at], right[c], ((1,), (0,))).astype(bf16)

    for copy in l_sib:
        copy.wait_recv()

    @pl.loop(0, CHUNKS)
    def _(r):
        at = aligned(r, size)
        eig[at] = dot(left[at], rot[...], ((1,), (0,))).astype(bf16)
        for i in range(1, nz):
            send(
                eig.at[at, aligned(plus(i), width)],
                ein.at[z, at],
                e_ss.at[i, r],
                e_rs.at[i, r],
                peer(dp, plus(i)),
            )
        local(eig.at[at, aligned(z, width)], ein.at[z, at], e_rs.at[0, r])

    @pl.loop(0, CHUNKS)
    def _(r):
        at = aligned(r, size)
        lhs = jnp.concatenate([grad[aligned(2 * j + c, width), :] for j in range(nz)], axis=0)
        out = dot(lhs, grad[at, :], ((1,), (1,))).astype(bf16)
        for j in range(nz):
            ggo[j, :, at] = out[j * width : (j + 1) * width]

    @pl.loop(0, CHUNKS)
    def _(r):
        at = aligned(r, size)
        lhs = jnp.concatenate([grad[:, aligned(2 * j + c, width)] for j in range(nz)], axis=1)
        out = dot(lhs, grad[:, at], ((0,), (0,))).astype(bf16)
        for j in range(nz):
            gto[j, :, at] = out[j * width : (j + 1) * width]

    load_first.wait()
    load_second.wait()

    @pl.loop(0, CHUNKS)
    def _(r):
        at = aligned(r, size)
        for i in list(range(1, nz)) + [0]:
            k = minus(i)
            piece = ein.at[k, at]
            pltpu.make_async_copy(piece, piece, e_rs.at[i, r]).wait()
            e = ein[k, at].astype(f32)
            new_first = first_beta * first[k, at] + (1.0 - first_beta) * e
            new_second = second_beta * second[k, at] + (1.0 - second_beta) * e * e
            nout[k, at] = (new_first / (jnp.sqrt(new_second) + epsilon)).astype(bf16)
            if i:
                send(
                    nout.at[k, at],
                    normed.at[at, aligned(z, width)],
                    n_ss.at[i, r],
                    n_rs.at[i, r],
                    peer(dp, k),
                )
            else:
                local(nout.at[k, at], normed.at[at, aligned(z, width)], n_rs.at[0, r])

    for i in range(nz):
        for r in range(CHUNKS):
            piece = normed.at[pl.ds(r * size, size), aligned(plus(i), width)]
            pltpu.make_async_copy(piece, piece, n_rs.at[i, r]).wait()

    def outer_send(out, into, ss, rs):
        copies = [
            send(out.at[plus(i)], into.at[z], ss.at[i], rs.at[i], peer(dp, plus(i)))
            for i in range(1, nz)
        ]
        return copies, local(out.at[z], into.at[z], rs.at[0])

    gg_copies, gg_own = outer_send(ggo, ggt_in, gg_ss, gg_rs)

    r_sib.wait_recv()

    @pl.loop(0, CHUNKS)
    def _(r):
        at = aligned(r, size)
        back[c, at] = dot(left[:, at], normed[...], ((0,), (0,))).astype(bf16)
        send(back.at[c, at], back.at[c, at], b_sib_ss.at[r], b_sib_rs.at[r], sibling)

    for r in range(CHUNKS):
        piece = back.at[1 - c, pl.ds(r * size, size)]
        pltpu.make_async_copy(piece, piece, b_sib_rs.at[r]).wait()

    per_chunk = n_dp // CHUNKS
    my_slot = dp * nz + z

    @pl.loop(0, CHUNKS)
    def _(r):
        rr = lax.rem(r + dp // per_chunk, CHUNKS)
        at = aligned(rr, size)
        total = None
        for p in range(2):
            rhs = jnp.concatenate(
                [right[p, aligned(2 * j + c, width), :] for j in range(nz)], axis=0
            )
            term = dot(back[p, at], rhs, ((1,), (1,)))
            total = term if total is None else total + term
        ucols[at] = total.astype(bf16)

        @pl.loop(0, per_chunk * nz)
        def _(q):
            dd = rr * per_chunk + lax.rem(dp + q // nz, per_chunk)
            j = lax.rem(z + q % nz, nz)
            src = ucols.at[aligned(dd, rows), aligned(j, width)]
            own = jnp.logical_and(dd == dp, j == z)

            @pl.when(own)
            def _():
                local(src, uin.at[my_slot], a_rs.at[1])

            @pl.when(jnp.logical_not(own))
            def _():
                send(src, uin.at[my_slot], a_ss.at[1], a_rs.at[1], peer(dd, j))

    gt_copies, gt_own = outer_send(gto, gtg_in, gt_ss, gt_rs)

    pltpu.make_async_copy(uin, uin, a_rs.at[1]).wait()

    @pl.loop(0, blocks)
    def _(b):
        upd[b] = uin[slot_ref[b]]

    for own, copies in ((gg_own, gg_copies), (gt_own, gt_copies)):
        own.wait()
        for copy in copies:
            copy.wait()
    for copies in (r_copies, l_copies, rs_copies, l_sib, g_sib, [r_sib]):
        for copy in copies:
            copy.wait_send()
    for i in turns:
        sib_copies[i].wait_send()
    sent = stage.at[pl.ds(0, devices - 1)]
    for n in range(2):
        pltpu.make_async_copy(sent, sent, a_ss.at[n]).wait()

    @pl.loop(0, CHUNKS)
    def _(r):
        at = aligned(r, size)
        for i in range(1, nz):
            piece = eig.at[at, aligned(plus(i), width)]
            pltpu.make_async_copy(piece, piece, e_ss.at[i, r]).wait()
            piece = nout.at[minus(i), at]
            pltpu.make_async_copy(piece, piece, n_ss.at[i, r]).wait()
        piece = back.at[c, at]
        pltpu.make_async_copy(piece, piece, b_sib_ss.at[r]).wait()


def run_step(slot_of_block, inverse, partial, left_basis, right_basis, first, second):
    blocks, rows, order = partial.shape
    nz, width = left_basis.shape[0], left_basis.shape[1]
    n_dp = lax.axis_size("dp")
    slots = n_dp * nz
    half = nz * width
    vmem = pl.BlockSpec(memory_space=pltpu.VMEM)
    smem = pl.BlockSpec(memory_space=pltpu.SMEM)
    anywhere = pl.BlockSpec(memory_space=pl.ANY)
    dma = pltpu.SemaphoreType.DMA
    scratch = [
        pltpu.VMEM((nz, blocks, rows, width), bf16),
        pltpu.VMEM((nz, blocks, rows, width), bf16),
        pltpu.VMEM((nz, blocks, rows, width), bf16),
        pltpu.VMEM((blocks + 1, rows, width), bf16),
        pltpu.VMEM((slots, rows, width), bf16),
        pltpu.VMEM((order, order), bf16),
        pltpu.VMEM((order, order), bf16),
        pltpu.VMEM((2, order, half), bf16),
        pltpu.VMEM((order, half), bf16),
        pltpu.VMEM((order, half), bf16),
        pltpu.VMEM((nz, order, width), f32),
        pltpu.VMEM((nz, order, width), f32),
        pltpu.VMEM((nz, order, width), bf16),
        pltpu.VMEM((order, half), bf16),
        pltpu.VMEM((2, order, half), bf16),
        pltpu.VMEM((nz, width, order), bf16),
        pltpu.VMEM((nz, width, order), bf16),
        pltpu.VMEM((order, half), bf16),
        pltpu.VMEM((slots, rows, width), bf16),
        dma((2,)),
        dma((nz,)),
        dma((nz,)),
        dma((nz,)),
        dma((nz,)),
        dma((nz,)),
        dma((2,)),
        dma((2,)),
        dma((nz,)),
        dma((nz,)),
        dma((nz,)),
        dma((nz,)),
        dma((nz,)),
        dma((nz,)),
        dma((nz,)),
        dma((nz,)),
        dma((nz, CHUNKS)),
        dma((nz, CHUNKS)),
        dma((nz, CHUNKS)),
        dma((nz, CHUNKS)),
        dma((nz,)),
        dma((nz,)),
        dma((nz,)),
        dma((nz,)),
        dma((CHUNKS,)),
        dma((CHUNKS,)),
        dma((1,)),
        dma((1,)),
    ]
    return pl.pallas_call(
        functools.partial(step_kernel, n_dp, nz),
        out_shape=(
            jax.ShapeDtypeStruct((blocks, rows, width), bf16),
            jax.ShapeDtypeStruct((nz, order, width), bf16),
            jax.ShapeDtypeStruct((nz, width, order), bf16),
            jax.ShapeDtypeStruct((nz, width, order), bf16),
        ),
        in_specs=[smem, smem] + [anywhere] * 5,
        out_specs=(vmem, vmem, vmem, vmem),
        scratch_shapes=scratch,
        compiler_params=pltpu.CompilerParams(
            collective_id=0, has_side_effects=True, vmem_limit_bytes=56 * 2**20
        ),
        cost_estimate=pl.CostEstimate(
            flops=12 * order * order * half, bytes_accessed=16 * 2**20, transcendentals=0
        ),
        name="soap_step",
    )(slot_of_block, inverse, partial, left_basis, right_basis, first, second)


def per_device(
    grad_partial,
    slot_of_block,
    left_factor,
    right_factor,
    left_basis,
    right_basis,
    first_moment,
    second_moment,
):
    blocks = grad_partial.shape[1]
    slots = lax.axis_size("dp") * left_factor.shape[0]
    slot_ids = jnp.arange(slots, dtype=jnp.int32)
    taken = slot_ids[:, None] == slot_of_block[None, :]
    offsets = jnp.arange(blocks, dtype=jnp.int32) - blocks
    inverse = blocks + jnp.sum(jnp.where(taken, offsets[None, :], 0), axis=1, dtype=jnp.int32)
    update, eigen, outer_left, outer_right = run_step(
        slot_of_block,
        inverse,
        grad_partial[0],
        left_basis,
        right_basis,
        first_moment,
        second_moment,
    )
    eigen = eigen.astype(f32)
    new_left = second_beta * left_factor + (1.0 - second_beta) * outer_left.astype(f32)
    new_right = second_beta * right_factor + (1.0 - second_beta) * outer_right.astype(f32)
    new_first = first_beta * first_moment + (1.0 - first_beta) * eigen
    new_second = second_beta * second_moment + (1.0 - second_beta) * eigen * eigen
    return (update, new_left, new_right, new_first, new_second)


def solution(mesh):
    in_specs = (
        P("tensor", None, "dp", None),
        P(),
        P("dp", "tensor", None),
        P("dp", "tensor", None),
        P("dp", "tensor", None),
        P("dp", None, "tensor"),
        P("dp", None, "tensor"),
        P("dp", None, "tensor"),
    )
    out_specs = (
        P(None, "dp", "tensor"),
        P("dp", "tensor", None),
        P("dp", "tensor", None),
        P("dp", None, "tensor"),
        P("dp", None, "tensor"),
    )
    return jax.shard_map(
        per_device, mesh=mesh, in_specs=in_specs, out_specs=out_specs, check_vma=False
    )
```

```python
import functools
import jax
import jax.numpy as jnp
from jax import lax
from jax.experimental import pallas as pl
from jax.experimental.pallas import tpu as pltpu
from jax.sharding import PartitionSpec as P

first_beta = 0.9
second_beta = 0.95
epsilon = 1e-08
f32 = jnp.float32
bf16 = jnp.bfloat16
CHUNKS = 4


def aligned(index, size):
    return pl.ds(pl.multiple_of(index * size, size), size)


def dot(a, b, dims):
    return lax.dot_general(a, b, (dims, ((), ())), preferred_element_type=f32)


def step_kernel(
    n_dp,
    nz,
    slot_ref,
    gp,
    lb,
    rb,
    left_hbm,
    right_hbm,
    first_hbm,
    second_hbm,
    upd,
    new_left,
    new_right,
    first,
    second,
    inv_ref,
    ein,
    ggt_in,
    gtg_in,
    mine,
    sibr,
    rsr,
    summed,
    stage,
    grad,
    left,
    right,
    rot,
    eig,
    nout,
    normed,
    back,
    ggo,
    gto,
    ucols,
    uin,
    load_sem,
    mine_sem,
    sib_ss,
    sib_rs,
    rs_ss,
    rs_rs,
    a_ss,
    a_rs,
    r_ss,
    r_rs,
    l_ss,
    l_rs,
    gg_ss,
    gg_rs,
    gt_ss,
    gt_rs,
    e_ss,
    e_rs,
    n_ss,
    n_rs,
    g_sib_ss,
    g_sib_rs,
    l_sib_ss,
    l_sib_rs,
    b_sib_ss,
    b_sib_rs,
    one_ss,
    one_rs,
    known,
):
    blocks, rows, order = gp.shape
    width = lb.shape[1]
    size = order // CHUNKS
    dp = lax.axis_index("dp")
    t = lax.axis_index("tensor")
    z = t // 2
    c = t % 2
    sibling = (dp, 2 * z + 1 - c)
    devices = n_dp * nz
    ny = n_dp // CHUNKS
    x = dp // ny
    y = dp % ny

    def peer(o, k):
        return (o, 2 * k + c)

    def send(src, dst, ss, rs, dev):
        copy = pltpu.make_async_remote_copy(
            src_ref=src,
            dst_ref=dst,
            send_sem=ss,
            recv_sem=rs,
            device_id=dev,
            device_id_type=pl.DeviceIdType.MESH,
        )
        copy.start()
        return copy

    def local(src, dst, sem):
        copy = pltpu.make_async_copy(src, dst, sem)
        copy.start()
        return copy

    def plus(i):
        return lax.rem(z + i, nz)

    def minus(i):
        return lax.rem(z + nz - i, nz)

    def partner(i):
        xx = lax.rem(x + i // (ny * nz), CHUNKS)
        yy = lax.rem(y + (i // nz) % ny, ny)
        return xx * ny + yy, lax.rem(z + i % nz, nz)

    def signal(sem, dev):
        pl.semaphore_signal(sem, inc=1, device_id=dev, device_id_type=pl.DeviceIdType.MESH)

    turns = (2, 1, nz - 1, 0)
    mine_copies = {}
    for i in turns:
        mine_copies[i] = local(
            gp.at[:, :, aligned(2 * plus(i) + c, width)], mine.at[i], mine_sem.at[i]
        )

    barrier = pltpu.get_barrier_semaphore()
    line_z = [peer(dp, plus(i)) for i in range(1, nz)]
    line_x = [peer(lax.rem(x + i, CHUNKS) * ny + y, z) for i in range(1, CHUNKS)]
    line_y = [peer(x * ny + lax.rem(y + i, ny), z) for i in range(1, ny)]
    greeted = [sibling] + line_z + line_x + line_y
    for dev in greeted:
        signal(barrier, dev)

    @pl.loop(0, devices)
    def _(i):
        found = jnp.int32(blocks)
        for b in range(blocks):
            found = jnp.where(slot_ref[b] == i, jnp.int32(b), found)
        inv_ref[i] = found

    pl.semaphore_wait(barrier, len(greeted))
    for dev in line_x:
        signal(known.at[0], dev)

    sib_copies = {}
    for i in turns:
        sib_copies[i] = send(
            gp.at[:, :, aligned(2 * plus(i) + 1 - c, width)],
            sibr.at[i],
            sib_ss.at[i],
            sib_rs.at[i],
            sibling,
        )

    r_copies = [
        send(
            rb.at[plus(i)],
            right.at[c, :, aligned(z, width)],
            r_ss.at[i],
            r_rs.at[i],
            peer(dp, plus(i)),
        )
        for i in range(1, nz)
    ]
    r_own = local(rb.at[z], right.at[c, :, aligned(z, width)], r_rs.at[0])

    step = 4
    part = blocks // 2
    low, high = pl.ds(0, part), pl.ds(part, part)

    def add(i, start, other):
        @pl.loop(0, part // step)
        def _(b):
            at = pl.ds(start + b * step, step)
            mine[i, at] = (mine[i, at].astype(f32) + other[at].astype(f32)).astype(bf16)

    def pass_on(i, at, into, n, hop):
        return send(mine.at[i, at], into, rs_ss.at[n], rs_rs.at[n], peer(dp, plus(hop)))

    def two_cores(i):
        mine_copies[i].wait()
        sib_copies[i].wait_recv()
        add(i, 0, sibr.at[i])
        add(i, part, sibr.at[i])

    last = nz - 1
    two_cores(2)
    pl.semaphore_wait(known.at[0], len(line_x))
    for dev in line_z:
        signal(known.at[1], dev)
    up = pass_on(2, low, rsr.at[0, low], 0, 1)
    down = pass_on(2, high, rsr.at[0, high], 1, last)
    two_cores(1)
    up_direct = pass_on(1, high, rsr.at[1, high], 2, 1)
    two_cores(last)
    down_direct = pass_on(last, low, rsr.at[2, low], 3, last)
    up.wait_recv()
    add(1, 0, rsr.at[0])
    up_sum = pass_on(1, low, rsr.at[1, low], 4, 1)
    down.wait_recv()
    add(last, part, rsr.at[0])
    down_sum = pass_on(last, high, rsr.at[2, high], 5, last)
    rs_copies = [up, down, up_direct, down_direct, up_sum, down_sum]
    mine_copies[0].wait()
    sib_copies[0].wait_recv()

    load_first = local(first_hbm, first, load_sem.at[0])
    load_second = local(second_hbm, second, load_sem.at[1])
    load_left = local(left_hbm, new_left, load_sem.at[2])
    load_right = local(right_hbm, new_right, load_sem.at[3])

    l_copies = [
        send(
            lb.at[plus(i)],
            left.at[aligned(2 * z + c, width)],
            l_ss.at[i],
            l_rs.at[i],
            peer(dp, plus(i)),
        )
        for i in range(1, nz)
    ]
    l_own = local(lb.at[z], left.at[aligned(2 * z + c, width)], l_rs.at[0])

    for copy in rs_copies[2:]:
        copy.wait_recv()

    @pl.loop(0, blocks // step)
    def _(b):
        at = pl.ds(b * step, step)
        total = mine[0, at].astype(f32) + sibr[0, at].astype(f32)
        total = total + rsr[1, at].astype(f32) + rsr[2, at].astype(f32)
        summed[at] = total.astype(bf16)

    summed[blocks] = jnp.zeros((rows, width), bf16)

    band = grad.at[c, aligned(dp, rows), aligned(z, width)]
    pl.semaphore_wait(known.at[1], len(line_z))

    def slot_rows(i):
        o, k = partner(i)
        stage[i] = summed[inv_ref[o * nz + k]]
        return o, k

    slot_rows(0)
    local(stage.at[0], band, a_rs.at[0])

    @pl.loop(1, devices)
    def _(i):
        o, k = slot_rows(i)
        send(stage.at[i], band, a_ss.at[0], a_rs.at[i // (ny * nz)], peer(o, k))

    r_own.wait()
    for copy in r_copies:
        copy.wait_recv()
    r_sib = send(right.at[c], right.at[c], one_ss.at[0], one_rs.at[0], sibling)
    l_own.wait()
    for copy in l_copies:
        copy.wait_recv()
    l_sib = []
    for j in range(nz):
        band = left.at[aligned(2 * j + c, width)]
        l_sib.append(send(band, band, l_sib_ss.at[j], l_sib_rs.at[j], sibling))

    def rotate(r):
        at = aligned(lax.rem(x + CHUNKS - r, CHUNKS), size)
        g_sib[r].wait_recv()
        total = None
        for p in range(2):
            rhs = jnp.concatenate(
                [right[c, pl.ds((2 * j + p) * width, width), :] for j in range(nz)], axis=0
            )
            term = dot(grad[p, at], rhs, ((1,), (0,)))
            total = term if total is None else total + term
        rot[at] = total.astype(bf16)

    g_sib = []
    for r in range(CHUNKS):
        piece = grad.at[c, aligned(lax.rem(x + CHUNKS - r, CHUNKS), size)]
        pltpu.make_async_copy(piece, piece, a_rs.at[r]).wait()
        g_sib.append(send(piece, piece, g_sib_ss.at[r], g_sib_rs.at[r], sibling))
        if r:
            rotate(r - 1)
    rotate(CHUNKS - 1)

    for copy in l_sib:
        copy.wait_recv()

    @pl.loop(0, CHUNKS)
    def _(r):
        at = aligned(r, size)
        eig[at] = dot(left[at], rot[...], ((1,), (0,))).astype(bf16)
        for i in range(1, nz):
            send(
                eig.at[at, aligned(plus(i), width)],
                ein.at[z, at],
                e_ss.at[i, r],
                e_rs.at[i, r],
                peer(dp, plus(i)),
            )
        local(eig.at[at, aligned(z, width)], ein.at[z, at], e_rs.at[0, r])

    @pl.loop(0, CHUNKS)
    def _(r):
        at = aligned(r, size)
        out = None
        for p in range(2):
            lhs = jnp.concatenate(
                [grad[p, aligned(2 * j + c, width), :] for j in range(nz)], axis=0
            )
            term = dot(lhs, grad[p, at], ((1,), (1,)))
            out = term if out is None else out + term
        out = out.astype(bf16)
        for j in range(nz):
            ggo[j, :, at] = out[j * width : (j + 1) * width]

    pair = nz // 2

    @pl.loop(0, 4)
    def _(r):
        p, h = r // 2, r % 2
        rhs = grad[p, :, aligned(h, pair * width)]
        out = dot(grad[c], rhs, ((0,), (0,))).astype(bf16)
        for j in range(nz):
            for n in range(pair):
                at = aligned(2 * (pair * h + n) + p, width)
                gto[j, :, at] = out[j * width : (j + 1) * width, n * width : (n + 1) * width]

    load_first.wait()
    load_second.wait()

    @pl.loop(0, CHUNKS)
    def _(r):
        at = aligned(r, size)
        for i in list(range(1, nz)) + [0]:
            k = minus(i)
            piece = ein.at[k, at]
            pltpu.make_async_copy(piece, piece, e_rs.at[i, r]).wait()
            e = ein[k, at].astype(f32)
            new_first = first_beta * first[k, at] + (1.0 - first_beta) * e
            new_second = second_beta * second[k, at] + (1.0 - second_beta) * e * e
            first[k, at] = new_first
            second[k, at] = new_second
            nout[k, at] = (new_first / (jnp.sqrt(new_second) + epsilon)).astype(bf16)
            if i:
                send(
                    nout.at[k, at],
                    normed.at[at, aligned(z, width)],
                    n_ss.at[i, r],
                    n_rs.at[i, r],
                    peer(dp, k),
                )
            else:
                local(nout.at[k, at], normed.at[at, aligned(z, width)], n_rs.at[0, r])

    def outer_send(out, into, ss, rs):
        copies = [
            send(out.at[plus(i)], into.at[z], ss.at[i], rs.at[i], peer(dp, plus(i)))
            for i in range(1, nz)
        ]
        return copies, local(out.at[z], into.at[z], rs.at[0])

    gg_copies, gg_own = outer_send(ggo, ggt_in, gg_ss, gg_rs)

    for i in range(nz):
        for r in range(CHUNKS):
            piece = normed.at[pl.ds(r * size, size), aligned(plus(i), width)]
            pltpu.make_async_copy(piece, piece, n_rs.at[i, r]).wait()

    r_sib.wait_recv()

    @pl.loop(0, CHUNKS)
    def _(r):
        at = aligned(r, size)
        back[c, at] = dot(left[:, at], normed[...], ((0,), (0,))).astype(bf16)
        send(back.at[c, at], back.at[c, at], b_sib_ss.at[r], b_sib_rs.at[r], sibling)

    for r in range(CHUNKS):
        piece = back.at[1 - c, pl.ds(r * size, size)]
        pltpu.make_async_copy(piece, piece, b_sib_rs.at[r]).wait()

    per_chunk = n_dp // CHUNKS
    my_slot = dp * nz + z

    @pl.loop(0, CHUNKS)
    def _(r):
        rr = lax.rem(r + dp // per_chunk, CHUNKS)
        at = aligned(rr, size)
        total = None
        for p in range(2):
            rhs = jnp.concatenate(
                [right[p, aligned(2 * j + c, width), :] for j in range(nz)], axis=0
            )
            term = dot(back[p, at], rhs, ((1,), (1,)))
            total = term if total is None else total + term
        ucols[at] = total.astype(bf16)

        @pl.loop(0, per_chunk * nz)
        def _(q):
            dd = rr * per_chunk + lax.rem(dp + q // nz, per_chunk)
            j = lax.rem(z + q % nz, nz)
            src = ucols.at[aligned(dd, rows), aligned(j, width)]
            own = jnp.logical_and(dd == dp, j == z)

            @pl.when(own)
            def _():
                local(src, uin.at[my_slot], a_rs.at[CHUNKS])

            @pl.when(jnp.logical_not(own))
            def _():
                send(src, uin.at[my_slot], a_ss.at[1], a_rs.at[CHUNKS], peer(dd, j))

    gt_copies, gt_own = outer_send(gto, gtg_in, gt_ss, gt_rs)

    def factors(load, into, outer, own, copies):
        load.wait()
        for i in range(nz):
            k = minus(i)
            (copies[i - 1].wait_recv if i else own.wait)()

            @pl.loop(0, width // 32)
            def _(b):
                at = pl.ds(b * 32, 32)
                into[k, at] = second_beta * into[k, at] + (1.0 - second_beta) * outer[
                    k, at
                ].astype(f32)

    factors(load_left, new_left, ggt_in, gg_own, gg_copies)
    pltpu.make_async_copy(uin, uin, a_rs.at[CHUNKS]).wait()

    @pl.loop(0, blocks)
    def _(b):
        upd[b] = uin[slot_ref[b]]

    factors(load_right, new_right, gtg_in, gt_own, gt_copies)

    for copies in (r_copies, l_copies, rs_copies, l_sib, g_sib, [r_sib], gg_copies, gt_copies):
        for copy in copies:
            copy.wait_send()
    for i in turns:
        sib_copies[i].wait_send()
    sent = stage.at[pl.ds(0, devices - 1)]
    for n in range(2):
        pltpu.make_async_copy(sent, sent, a_ss.at[n]).wait()

    @pl.loop(0, CHUNKS)
    def _(r):
        at = aligned(r, size)
        for i in range(1, nz):
            piece = eig.at[at, aligned(plus(i), width)]
            pltpu.make_async_copy(piece, piece, e_ss.at[i, r]).wait()
            piece = nout.at[minus(i), at]
            pltpu.make_async_copy(piece, piece, n_ss.at[i, r]).wait()
        piece = back.at[c, at]
        pltpu.make_async_copy(piece, piece, b_sib_ss.at[r]).wait()


def run_step(
    slot_of_block, partial, left_basis, right_basis, left_factor, right_factor, first, second
):
    blocks, rows, order = partial.shape
    nz, width = left_basis.shape[0], left_basis.shape[1]
    n_dp = lax.axis_size("dp")
    slots = n_dp * nz
    half = nz * width
    large = (partial, left_basis, right_basis, left_factor, right_factor, first, second)
    large = [pltpu.with_memory_space_constraint(array, pltpu.HBM) for array in large]
    vmem = pl.BlockSpec(memory_space=pltpu.VMEM)
    smem = pl.BlockSpec(memory_space=pltpu.SMEM)
    hbm = pl.BlockSpec(memory_space=pltpu.HBM)
    dma = pltpu.SemaphoreType.DMA
    scratch = [
        pltpu.SMEM((slots,), jnp.int32),
        pltpu.VMEM((nz, order, width), bf16),
        pltpu.VMEM((nz, width, order), bf16),
        pltpu.VMEM((nz, width, order), bf16),
        pltpu.VMEM((nz, blocks, rows, width), bf16),
        pltpu.VMEM((nz, blocks, rows, width), bf16),
        pltpu.VMEM((3, blocks, rows, width), bf16),
        pltpu.VMEM((blocks + 1, rows, width), bf16),
        pltpu.VMEM((slots, rows, width), bf16),
        pltpu.VMEM((2, order, half), bf16),
        pltpu.VMEM((order, order), bf16),
        pltpu.VMEM((2, order, half), bf16),
        pltpu.VMEM((order, half), bf16),
        pltpu.VMEM((order, half), bf16),
        pltpu.VMEM((nz, order, width), bf16),
        pltpu.VMEM((order, half), bf16),
        pltpu.VMEM((2, order, half), bf16),
        pltpu.VMEM((nz, width, order), bf16),
        pltpu.VMEM((nz, width, order), bf16),
        pltpu.VMEM((order, half), bf16),
        pltpu.VMEM((slots, rows, width), bf16),
        dma((4,)),
        dma((nz,)),
        dma((nz,)),
        dma((nz,)),
        dma((6,)),
        dma((6,)),
        dma((2,)),
        dma((CHUNKS + 1,)),
        dma((nz,)),
        dma((nz,)),
        dma((nz,)),
        dma((nz,)),
        dma((nz,)),
        dma((nz,)),
        dma((nz,)),
        dma((nz,)),
        dma((nz, CHUNKS)),
        dma((nz, CHUNKS)),
        dma((nz, CHUNKS)),
        dma((nz, CHUNKS)),
        dma((CHUNKS,)),
        dma((CHUNKS,)),
        dma((nz,)),
        dma((nz,)),
        dma((CHUNKS,)),
        dma((CHUNKS,)),
        dma((1,)),
        dma((1,)),
        pltpu.SemaphoreType.REGULAR((2,)),
    ]
    return pl.pallas_call(
        functools.partial(step_kernel, n_dp, nz),
        out_shape=(
            jax.ShapeDtypeStruct((blocks, rows, width), bf16),
            jax.ShapeDtypeStruct((nz, width, order), f32),
            jax.ShapeDtypeStruct((nz, width, order), f32),
            jax.ShapeDtypeStruct((nz, order, width), f32),
            jax.ShapeDtypeStruct((nz, order, width), f32),
        ),
        in_specs=[smem] + [hbm] * 7,
        out_specs=(vmem,) * 5,
        scratch_shapes=scratch,
        compiler_params=pltpu.CompilerParams(
            collective_id=0, has_side_effects=True, vmem_limit_bytes=40 * 2**20
        ),
        cost_estimate=pl.CostEstimate(
            flops=12 * order * order * half, bytes_accessed=16 * 2**20, transcendentals=0
        ),
        name="soap_step",
    )(slot_of_block, *large)


def per_device(
    grad_partial,
    slot_of_block,
    left_factor,
    right_factor,
    left_basis,
    right_basis,
    first_moment,
    second_moment,
):
    return run_step(
        slot_of_block,
        grad_partial[0],
        left_basis,
        right_basis,
        left_factor,
        right_factor,
        first_moment,
        second_moment,
    )


def solution(mesh):
    in_specs = (
        P("tensor", None, "dp", None),
        P(),
        P("dp", "tensor", None),
        P("dp", "tensor", None),
        P("dp", "tensor", None),
        P("dp", None, "tensor"),
        P("dp", None, "tensor"),
        P("dp", None, "tensor"),
    )
    out_specs = (
        P(None, "dp", "tensor"),
        P("dp", "tensor", None),
        P("dp", "tensor", None),
        P("dp", None, "tensor"),
        P("dp", None, "tensor"),
    )
    return jax.shard_map(
        per_device, mesh=mesh, in_specs=in_specs, out_specs=out_specs, check_vma=False
    )
```

```python
import functools
import jax
import jax.numpy as jnp
from jax import lax
from jax.experimental import pallas as pl
from jax.experimental.pallas import tpu as pltpu
from jax.sharding import PartitionSpec as P

first_beta = 0.9
second_beta = 0.95
epsilon = 1e-08
f32 = jnp.float32
bf16 = jnp.bfloat16
CHUNKS = 4


def aligned(index, size):
    return pl.ds(pl.multiple_of(index * size, size), size)


def dot(a, b, dims):
    return lax.dot_general(a, b, (dims, ((), ())), preferred_element_type=f32)


def step_kernel(
    n_dp,
    nz,
    slot_hbm,
    gp,
    lb,
    rb,
    left_hbm,
    right_hbm,
    first_hbm,
    second_hbm,
    upd,
    new_left,
    new_right,
    first,
    second,
    slot_ref,
    inv_ref,
    ein,
    ggt_in,
    gtg_in,
    mine,
    sibr,
    rsr,
    summed,
    stage,
    grad,
    left,
    right,
    rot,
    eig,
    nout,
    normed,
    back,
    ggo,
    gto,
    ucols,
    uin,
    load_sem,
    mine_sem,
    sib_ss,
    sib_rs,
    rs_ss,
    rs_rs,
    a_ss,
    a_rs,
    r_ss,
    r_rs,
    l_ss,
    l_rs,
    gg_ss,
    gg_rs,
    gt_ss,
    gt_rs,
    e_ss,
    e_rs,
    n_ss,
    n_rs,
    g_sib_ss,
    g_sib_rs,
    l_sib_ss,
    l_sib_rs,
    b_sib_ss,
    b_sib_rs,
    one_ss,
    one_rs,
    known,
):
    blocks, rows, order = gp.shape
    width = lb.shape[1]
    size = order // CHUNKS
    band_size = width // CHUNKS
    band_half = width // 2
    dp = lax.axis_index("dp")
    t = lax.axis_index("tensor")
    z = t // 2
    c = t % 2
    sibling = (dp, 2 * z + 1 - c)
    devices = n_dp * nz
    ny = n_dp // CHUNKS
    x = dp // ny
    y = dp % ny

    def peer(o, k):
        return (o, 2 * k + c)

    def send(src, dst, ss, rs, dev):
        copy = pltpu.make_async_remote_copy(
            src_ref=src,
            dst_ref=dst,
            send_sem=ss,
            recv_sem=rs,
            device_id=dev,
            device_id_type=pl.DeviceIdType.MESH,
        )
        copy.start()
        return copy

    def local(src, dst, sem):
        copy = pltpu.make_async_copy(src, dst, sem)
        copy.start()
        return copy

    def plus(i):
        return lax.rem(z + i, nz)

    def minus(i):
        return lax.rem(z + nz - i, nz)

    def partner(i):
        xx = lax.rem(x + i // (ny * nz), CHUNKS)
        yy = lax.rem(y + (i // nz) % ny, ny)
        return xx * ny + yy, lax.rem(z + i % nz, nz)

    def signal(sem, dev):
        pl.semaphore_signal(sem, inc=1, device_id=dev, device_id_type=pl.DeviceIdType.MESH)

    slot_copy = local(slot_hbm, slot_ref, load_sem.at[4])
    turns = (2, 1, nz - 1, 0)
    mine_copies = {}
    for i in turns:
        mine_copies[i] = local(
            gp.at[:, :, aligned(2 * plus(i) + c, width)], mine.at[i], mine_sem.at[i]
        )

    barrier = pltpu.get_barrier_semaphore()
    line_z = [peer(dp, plus(i)) for i in range(1, nz)]
    line_x = [peer(lax.rem(x + i, CHUNKS) * ny + y, z) for i in range(1, CHUNKS)]
    line_y = [peer(x * ny + lax.rem(y + i, ny), z) for i in range(1, ny)]
    greeted = [sibling] + line_z + line_x + line_y
    for dev in greeted:
        signal(barrier, dev)

    slot_copy.wait()
    @pl.loop(0, devices)
    def _(i):
        found = jnp.int32(blocks)
        for b in range(blocks):
            found = jnp.where(slot_ref[b] == i, jnp.int32(b), found)
        inv_ref[i] = found

    pl.semaphore_wait(barrier, len(greeted))
    for dev in line_x:
        signal(known.at[0], dev)

    sib_copies = {}
    for i in turns:
        sib_copies[i] = send(
            gp.at[:, :, aligned(2 * plus(i) + 1 - c, width)],
            sibr.at[i],
            sib_ss.at[i],
            sib_rs.at[i],
            sibling,
        )

    r_copies = [
        send(
            rb.at[plus(i)],
            right.at[c, :, aligned(z, width)],
            r_ss.at[i],
            r_rs.at[i],
            peer(dp, plus(i)),
        )
        for i in range(1, nz)
    ]
    r_own = local(rb.at[z], right.at[c, :, aligned(z, width)], r_rs.at[0])

    step = 4
    part = blocks // 2
    low, high = pl.ds(0, part), pl.ds(part, part)

    def add(i, start, other):
        @pl.loop(0, part // step)
        def _(b):
            at = pl.ds(start + b * step, step)
            mine[i, at] = (mine[i, at].astype(f32) + other[at].astype(f32)).astype(bf16)

    def pass_on(i, at, into, n, hop):
        return send(mine.at[i, at], into, rs_ss.at[n], rs_rs.at[n], peer(dp, plus(hop)))

    def two_cores(i):
        mine_copies[i].wait()
        sib_copies[i].wait_recv()
        add(i, 0, sibr.at[i])
        add(i, part, sibr.at[i])

    last = nz - 1
    two_cores(2)
    pl.semaphore_wait(known.at[0], len(line_x))
    for dev in line_z:
        signal(known.at[1], dev)
    up = pass_on(2, low, rsr.at[0, low], 0, 1)
    down = pass_on(2, high, rsr.at[0, high], 1, last)
    two_cores(1)
    up_direct = pass_on(1, high, rsr.at[1, high], 2, 1)
    two_cores(last)
    down_direct = pass_on(last, low, rsr.at[2, low], 3, last)
    up.wait_recv()
    add(1, 0, rsr.at[0])
    up_sum = pass_on(1, low, rsr.at[1, low], 4, 1)
    down.wait_recv()
    add(last, part, rsr.at[0])
    down_sum = pass_on(last, high, rsr.at[2, high], 5, last)
    rs_copies = [up, down, up_direct, down_direct, up_sum, down_sum]
    mine_copies[0].wait()
    sib_copies[0].wait_recv()

    load_first = local(first_hbm, first, load_sem.at[0])
    load_second = local(second_hbm, second, load_sem.at[1])
    load_left = local(left_hbm, new_left, load_sem.at[2])
    load_right = local(right_hbm, new_right, load_sem.at[3])

    def left_part(h):
        at = pl.ds(h * band_half, band_half)
        band = left.at[z, c, at]
        copies = [
            send(
                lb.at[plus(i), at], band, l_ss.at[h, i], l_rs.at[h, i], peer(dp, plus(i))
            )
            for i in range(1, nz)
        ]
        return copies, local(lb.at[z, at], band, l_rs.at[h, 0])

    def left_sibling(h, copies, own):
        own.wait()
        for copy in copies:
            copy.wait_recv()
        bands = left.at[:, c, pl.ds(h * band_half, band_half)]
        return send(bands, bands, l_sib_ss.at[h], l_sib_rs.at[h], sibling)

    l_copies, l_own = left_part(0)

    for copy in rs_copies[2:]:
        copy.wait_recv()

    @pl.loop(0, blocks // step)
    def _(b):
        at = pl.ds(b * step, step)
        total = mine[0, at].astype(f32) + sibr[0, at].astype(f32)
        total = total + rsr[1, at].astype(f32) + rsr[2, at].astype(f32)
        summed[at] = total.astype(bf16)

    summed[blocks] = jnp.zeros((rows, width), bf16)

    band = grad.at[c, aligned(dp, rows), aligned(z, width)]
    pl.semaphore_wait(known.at[1], len(line_z))

    def slot_rows(i):
        o, k = partner(i)
        stage[i] = summed[inv_ref[o * nz + k]]
        return o, k

    slot_rows(0)
    local(stage.at[0], band, a_rs.at[0])

    @pl.loop(1, devices)
    def _(i):
        o, k = slot_rows(i)
        send(stage.at[i], band, a_ss.at[0], a_rs.at[i // (ny * nz)], peer(o, k))

    r_own.wait()
    for copy in r_copies:
        copy.wait_recv()
    r_sib = send(right.at[c], right.at[c], one_ss.at[0], one_rs.at[0], sibling)
    l_sib = [left_sibling(0, l_copies, l_own)]

    def rotate(r):
        at = aligned(lax.rem(x + CHUNKS - r, CHUNKS), size)
        g_sib[r].wait_recv()
        total = None
        for p in range(2):
            rhs = jnp.concatenate(
                [right[c, pl.ds((2 * j + p) * width, width), :] for j in range(nz)], axis=0
            )
            term = dot(grad[p, at], rhs, ((1,), (0,)))
            total = term if total is None else total + term
        rot[at] = total.astype(bf16)

    g_sib = []
    for r in range(CHUNKS):
        piece = grad.at[c, aligned(lax.rem(x + CHUNKS - r, CHUNKS), size)]
        pltpu.make_async_copy(piece, piece, a_rs.at[r]).wait()
        g_sib.append(send(piece, piece, g_sib_ss.at[r], g_sib_rs.at[r], sibling))
        if r:
            rotate(r - 1)
    l_copies_more, l_own = left_part(1)
    rotate(CHUNKS - 1)

    def eigen(r):
        at = aligned(r, band_size)
        lhs = left[:, :, at, :].reshape(size, order)
        out = dot(lhs, rot[...], ((1,), (0,))).astype(bf16)
        eig[:, at, :] = out.reshape(2 * nz, band_size, nz * width)
        for i in range(1, nz):
            send(
                eig.at[:, at, aligned(plus(i), width)],
                ein.at[z, :, at],
                e_ss.at[i, r],
                e_rs.at[i, r],
                peer(dp, plus(i)),
            )
        local(eig.at[:, at, aligned(z, width)], ein.at[z, :, at], e_rs.at[0, r])

    l_sib[0].wait_recv()
    pl.loop(0, CHUNKS // 2)(eigen)
    l_sib.append(left_sibling(1, l_copies_more, l_own))
    l_sib[1].wait_recv()
    pl.loop(CHUNKS // 2, CHUNKS)(eigen)

    @pl.loop(0, CHUNKS)
    def _(r):
        at = aligned(r, size)
        out = None
        for p in range(2):
            lhs = jnp.concatenate(
                [grad[p, aligned(2 * j + c, width), :] for j in range(nz)], axis=0
            )
            term = dot(lhs, grad[p, at], ((1,), (1,)))
            out = term if out is None else out + term
        out = out.astype(bf16)
        for j in range(nz):
            ggo[j, :, at] = out[j * width : (j + 1) * width]

    pair = nz // 2

    @pl.loop(0, 4)
    def _(r):
        p, h = r // 2, r % 2
        rhs = grad[p, :, aligned(h, pair * width)]
        out = dot(grad[c], rhs, ((0,), (0,))).astype(bf16)
        for j in range(nz):
            for n in range(pair):
                at = aligned(2 * (pair * h + n) + p, width)
                gto[j, :, at] = out[j * width : (j + 1) * width, n * width : (n + 1) * width]

    load_first.wait()
    load_second.wait()

    @pl.loop(0, CHUNKS)
    def _(r):
        at = aligned(r, band_size)
        for i in list(range(1, nz)) + [0]:
            k = minus(i)
            piece = ein.at[k, :, at]
            pltpu.make_async_copy(piece, piece, e_rs.at[i, r]).wait()
            e = ein[k, :, at].astype(f32)
            new_first = first_beta * first[k, :, at] + (1.0 - first_beta) * e
            new_second = second_beta * second[k, :, at] + (1.0 - second_beta) * e * e
            first[k, :, at] = new_first
            second[k, :, at] = new_second
            nout[k, :, at] = (new_first / (jnp.sqrt(new_second) + epsilon)).astype(bf16)
            if i:
                send(
                    nout.at[k, :, at],
                    normed.at[:, at, aligned(z, width)],
                    n_ss.at[i, r],
                    n_rs.at[i, r],
                    peer(dp, k),
                )
            else:
                local(nout.at[k, :, at], normed.at[:, at, aligned(z, width)], n_rs.at[0, r])

    def outer_send(out, into, ss, rs):
        copies = [
            send(out.at[plus(i)], into.at[z], ss.at[i], rs.at[i], peer(dp, plus(i)))
            for i in range(1, nz)
        ]
        return copies, local(out.at[z], into.at[z], rs.at[0])

    gg_copies, gg_own = outer_send(ggo, ggt_in, gg_ss, gg_rs)

    for i in range(nz):
        for r in range(CHUNKS):
            piece = normed.at[:, pl.ds(r * band_size, band_size), aligned(plus(i), width)]
            pltpu.make_async_copy(piece, piece, n_rs.at[i, r]).wait()

    r_sib.wait_recv()

    @pl.loop(0, CHUNKS)
    def _(r):
        at = aligned(r, size)
        lhs = left[:, :, :, at].reshape(order, size)
        rhs = normed[...].reshape(order, nz * width)
        back[c, at] = dot(lhs, rhs, ((0,), (0,))).astype(bf16)
        send(back.at[c, at], back.at[c, at], b_sib_ss.at[r], b_sib_rs.at[r], sibling)

    for r in range(CHUNKS):
        piece = back.at[1 - c, pl.ds(r * size, size)]
        pltpu.make_async_copy(piece, piece, b_sib_rs.at[r]).wait()

    per_chunk = n_dp // CHUNKS
    my_slot = dp * nz + z

    @pl.loop(0, CHUNKS)
    def _(r):
        rr = lax.rem(r + dp // per_chunk, CHUNKS)
        at = aligned(rr, size)
        total = None
        for p in range(2):
            rhs = jnp.concatenate(
                [right[p, aligned(2 * j + c, width), :] for j in range(nz)], axis=0
            )
            term = dot(back[p, at], rhs, ((1,), (1,)))
            total = term if total is None else total + term
        ucols[at] = total.astype(bf16)

        @pl.loop(0, per_chunk * nz)
        def _(q):
            dd = rr * per_chunk + lax.rem(dp + q // nz, per_chunk)
            j = lax.rem(z + q % nz, nz)
            src = ucols.at[aligned(dd, rows), aligned(j, width)]
            own = jnp.logical_and(dd == dp, j == z)

            @pl.when(own)
            def _():
                local(src, uin.at[my_slot], a_rs.at[CHUNKS])

            @pl.when(jnp.logical_not(own))
            def _():
                send(src, uin.at[my_slot], a_ss.at[1], a_rs.at[CHUNKS], peer(dd, j))

    gt_copies, gt_own = outer_send(gto, gtg_in, gt_ss, gt_rs)

    def factors(load, into, outer, own, copies):
        load.wait()
        for i in range(nz):
            k = minus(i)
            (copies[i - 1].wait_recv if i else own.wait)()

            @pl.loop(0, width // 32)
            def _(b):
                at = pl.ds(b * 32, 32)
                into[k, at] = second_beta * into[k, at] + (1.0 - second_beta) * outer[
                    k, at
                ].astype(f32)

    factors(load_left, new_left, ggt_in, gg_own, gg_copies)
    pltpu.make_async_copy(uin, uin, a_rs.at[CHUNKS]).wait()

    @pl.loop(0, blocks)
    def _(b):
        upd[b] = uin[slot_ref[b]]

    factors(load_right, new_right, gtg_in, gt_own, gt_copies)

    for copies in (r_copies, l_copies, l_copies_more, rs_copies, l_sib, g_sib, [r_sib], gg_copies, gt_copies):
        for copy in copies:
            copy.wait_send()
    for i in turns:
        sib_copies[i].wait_send()
    sent = stage.at[pl.ds(0, devices - 1)]
    for n in range(2):
        pltpu.make_async_copy(sent, sent, a_ss.at[n]).wait()

    @pl.loop(0, CHUNKS)
    def _(r):
        at, band = aligned(r, size), aligned(r, band_size)
        for i in range(1, nz):
            piece = eig.at[:, band, aligned(plus(i), width)]
            pltpu.make_async_copy(piece, piece, e_ss.at[i, r]).wait()
            piece = nout.at[minus(i), :, band]
            pltpu.make_async_copy(piece, piece, n_ss.at[i, r]).wait()
        piece = back.at[c, at]
        pltpu.make_async_copy(piece, piece, b_sib_ss.at[r]).wait()


def write_out(*refs):
    count = len(refs) // 2
    sems = refs[-1]
    copies = []
    for n in range(count):
        for k in range(sems.shape[1]):
            share = refs[n].shape[0] // sems.shape[1]
            at = pl.ds(k * share, share)
            copy = pltpu.make_async_copy(refs[n].at[at], refs[count + n].at[at], sems.at[n, k])
            copy.start()
            copies.append(copy)
    for copy in copies:
        copy.wait()


def by_band(array):
    slots, order, width = array.shape
    return array.reshape(slots, order // width, width, width)


def run_step(
    slot_of_block, partial, left_basis, right_basis, left_factor, right_factor, first, second
):
    blocks, rows, order = partial.shape
    nz, width = left_basis.shape[0], left_basis.shape[1]
    n_dp = lax.axis_size("dp")
    slots = n_dp * nz
    half = nz * width
    operands = (slot_of_block, partial, left_basis, right_basis)
    operands += (left_factor, right_factor, by_band(first), by_band(second))
    operands = [pltpu.with_memory_space_constraint(array, pltpu.HBM) for array in operands]
    vmem = pl.BlockSpec(memory_space=pltpu.VMEM)
    hbm = pl.BlockSpec(memory_space=pltpu.HBM)
    dma = pltpu.SemaphoreType.DMA
    scratch = [
        pltpu.SMEM(slot_of_block.shape, jnp.int32),
        pltpu.SMEM((slots,), jnp.int32),
        pltpu.VMEM((nz, 2 * nz, width, width), bf16),
        pltpu.VMEM((nz, width, order), bf16),
        pltpu.VMEM((nz, width, order), bf16),
        pltpu.VMEM((nz, blocks, rows, width), bf16),
        pltpu.VMEM((nz, blocks, rows, width), bf16),
        pltpu.VMEM((3, blocks, rows, width), bf16),
        pltpu.VMEM((blocks + 1, rows, width), bf16),
        pltpu.VMEM((slots, rows, width), bf16),
        pltpu.VMEM((2, order, half), bf16),
        pltpu.VMEM((nz, 2, width, order), bf16),
        pltpu.VMEM((2, order, half), bf16),
        pltpu.VMEM((order, half), bf16),
        pltpu.VMEM((2 * nz, width, half), bf16),
        pltpu.VMEM((nz, 2 * nz, width, width), bf16),
        pltpu.VMEM((2 * nz, width, half), bf16),
        pltpu.VMEM((2, order, half), bf16),
        pltpu.VMEM((nz, width, order), bf16),
        pltpu.VMEM((nz, width, order), bf16),
        pltpu.VMEM((order, half), bf16),
        pltpu.VMEM((slots, rows, width), bf16),
        dma((5,)),
        dma((nz,)),
        dma((nz,)),
        dma((nz,)),
        dma((6,)),
        dma((6,)),
        dma((2,)),
        dma((CHUNKS + 1,)),
        dma((nz,)),
        dma((nz,)),
        dma((2, nz)),
        dma((2, nz)),
        dma((nz,)),
        dma((nz,)),
        dma((nz,)),
        dma((nz,)),
        dma((nz, CHUNKS)),
        dma((nz, CHUNKS)),
        dma((nz, CHUNKS)),
        dma((nz, CHUNKS)),
        dma((CHUNKS,)),
        dma((CHUNKS,)),
        dma((2,)),
        dma((2,)),
        dma((CHUNKS,)),
        dma((CHUNKS,)),
        dma((1,)),
        dma((1,)),
        pltpu.SemaphoreType.REGULAR((2,)),
    ]
    results = pl.pallas_call(
        functools.partial(step_kernel, n_dp, nz),
        out_shape=(
            jax.ShapeDtypeStruct((blocks, rows, width), bf16),
            jax.ShapeDtypeStruct((nz, width, order), f32),
            jax.ShapeDtypeStruct((nz, width, order), f32),
            jax.ShapeDtypeStruct((nz, 2 * nz, width, width), f32),
            jax.ShapeDtypeStruct((nz, 2 * nz, width, width), f32),
        ),
        in_specs=[hbm] * 8,
        out_specs=(vmem,) * 5,
        scratch_shapes=scratch,
        compiler_params=pltpu.CompilerParams(
            collective_id=0, has_side_effects=True, vmem_limit_bytes=40 * 2**20
        ),
        cost_estimate=pl.CostEstimate(
            flops=12 * order * order * half, bytes_accessed=16 * 2**20, transcendentals=0
        ),
        name="soap_step",
    )(*operands)
    update, new_left, new_right, new_first, new_second = pl.pallas_call(
        write_out,
        out_shape=[jax.ShapeDtypeStruct(array.shape, array.dtype) for array in results],
        in_specs=[pl.BlockSpec(memory_space=pl.ANY)] * 5,
        out_specs=[hbm] * 5,
        scratch_shapes=[dma((5, 4))],
        compiler_params=pltpu.CompilerParams(vmem_limit_bytes=2**20),
        name="write_out",
    )(*results)
    return update, new_left, new_right, new_first.reshape(first.shape), new_second.reshape(first.shape)


def per_device(
    grad_partial,
    slot_of_block,
    left_factor,
    right_factor,
    left_basis,
    right_basis,
    first_moment,
    second_moment,
):
    return run_step(
        slot_of_block,
        grad_partial[0],
        left_basis,
        right_basis,
        left_factor,
        right_factor,
        first_moment,
        second_moment,
    )


def solution(mesh):
    in_specs = (
        P("tensor", None, "dp", None),
        P(),
        P("dp", "tensor", None),
        P("dp", "tensor", None),
        P("dp", "tensor", None),
        P("dp", None, "tensor"),
        P("dp", None, "tensor"),
        P("dp", None, "tensor"),
    )
    out_specs = (
        P(None, "dp", "tensor"),
        P("dp", "tensor", None),
        P("dp", "tensor", None),
        P("dp", None, "tensor"),
        P("dp", None, "tensor"),
    )
    return jax.shard_map(
        per_device, mesh=mesh, in_specs=in_specs, out_specs=out_specs, check_vma=False
    )
```

```python
import functools
import jax
import jax.numpy as jnp
from jax import lax
from jax.experimental import pallas as pl
from jax.experimental.pallas import tpu as pltpu
from jax.sharding import PartitionSpec as P

first_beta = 0.9
second_beta = 0.95
epsilon = 1e-08
f32 = jnp.float32
bf16 = jnp.bfloat16
CHUNKS = 4


def aligned(index, size):
    return pl.ds(pl.multiple_of(index * size, size), size)


def dot(a, b, dims):
    return lax.dot_general(a, b, (dims, ((), ())), preferred_element_type=f32)


def step_kernel(
    n_dp,
    nz,
    slot_hbm,
    gp,
    lb,
    rb,
    left_hbm,
    right_hbm,
    first_hbm,
    second_hbm,
    upd,
    new_left,
    new_right,
    first,
    second,
    slot_ref,
    inv_ref,
    ein,
    ggt_in,
    gtg_in,
    mine,
    sibr,
    rsr,
    summed,
    stage,
    grad,
    left,
    right,
    rot,
    eig,
    nout,
    normed,
    back,
    ggo,
    gto,
    ucols,
    uin,
    load_sem,
    mine_sem,
    sib_ss,
    sib_rs,
    rs_ss,
    rs_rs,
    a_ss,
    a_rs,
    r_ss,
    r_rs,
    l_ss,
    l_rs,
    gg_ss,
    gg_rs,
    gt_ss,
    gt_rs,
    e_ss,
    e_rs,
    n_ss,
    n_rs,
    g_sib_ss,
    g_sib_rs,
    l_sib_ss,
    l_sib_rs,
    b_sib_ss,
    b_sib_rs,
    one_ss,
    one_rs,
    known,
):
    blocks, rows, order = gp.shape
    width = lb.shape[1]
    size = order // CHUNKS
    band_size = width // CHUNKS
    shares = (pl.ds(0, 3 * band_size), pl.ds(3 * band_size, band_size))
    dp = lax.axis_index("dp")
    t = lax.axis_index("tensor")
    z = t // 2
    c = t % 2
    sibling = (dp, 2 * z + 1 - c)
    devices = n_dp * nz
    ny = n_dp // CHUNKS
    x = dp // ny
    y = dp % ny

    def peer(o, k):
        return (o, 2 * k + c)

    def send(src, dst, ss, rs, dev):
        copy = pltpu.make_async_remote_copy(
            src_ref=src,
            dst_ref=dst,
            send_sem=ss,
            recv_sem=rs,
            device_id=dev,
            device_id_type=pl.DeviceIdType.MESH,
        )
        copy.start()
        return copy

    def local(src, dst, sem):
        copy = pltpu.make_async_copy(src, dst, sem)
        copy.start()
        return copy

    def plus(i):
        return lax.rem(z + i, nz)

    def minus(i):
        return lax.rem(z + nz - i, nz)

    def partner(i):
        xx = lax.rem(x + i // (ny * nz), CHUNKS)
        yy = lax.rem(y + (i // nz) % ny, ny)
        return xx * ny + yy, lax.rem(z + i % nz, nz)

    def signal(sem, dev):
        pl.semaphore_signal(sem, inc=1, device_id=dev, device_id_type=pl.DeviceIdType.MESH)

    slot_copy = local(slot_hbm, slot_ref, load_sem.at[4])
    turns = (2, 1, nz - 1, 0)
    mine_copies = {}
    for i in turns:
        mine_copies[i] = local(
            gp.at[:, :, aligned(2 * plus(i) + c, width)], mine.at[i], mine_sem.at[i]
        )

    barrier = pltpu.get_barrier_semaphore()
    line_z = [peer(dp, plus(i)) for i in range(1, nz)]
    line_x = [peer(lax.rem(x + i, CHUNKS) * ny + y, z) for i in range(1, CHUNKS)]
    line_y = [peer(x * ny + lax.rem(y + i, ny), z) for i in range(1, ny)]
    greeted = [sibling] + line_z + line_x + line_y
    for dev in greeted:
        signal(barrier, dev)

    slot_copy.wait()
    @pl.loop(0, devices)
    def _(i):
        found = jnp.int32(blocks)
        for b in range(blocks):
            found = jnp.where(slot_ref[b] == i, jnp.int32(b), found)
        inv_ref[i] = found

    pl.semaphore_wait(barrier, len(greeted))
    for dev in line_x:
        signal(known.at[0], dev)

    sib_copies = {}
    for i in turns:
        sib_copies[i] = send(
            gp.at[:, :, aligned(2 * plus(i) + 1 - c, width)],
            sibr.at[i],
            sib_ss.at[i],
            sib_rs.at[i],
            sibling,
        )

    r_copies = [
        send(
            rb.at[plus(i)],
            right.at[c, :, aligned(z, width)],
            r_ss.at[i],
            r_rs.at[i],
            peer(dp, plus(i)),
        )
        for i in range(1, nz)
    ]
    r_own = local(rb.at[z], right.at[c, :, aligned(z, width)], r_rs.at[0])

    step = 4
    part = blocks // 2
    low, high = pl.ds(0, part), pl.ds(part, part)

    def add(i, start, other):
        @pl.loop(0, part // step)
        def _(b):
            at = pl.ds(start + b * step, step)
            mine[i, at] = (mine[i, at].astype(f32) + other[at].astype(f32)).astype(bf16)

    def pass_on(i, at, into, n, hop):
        return send(mine.at[i, at], into, rs_ss.at[n], rs_rs.at[n], peer(dp, plus(hop)))

    def two_cores(i):
        mine_copies[i].wait()
        sib_copies[i].wait_recv()
        add(i, 0, sibr.at[i])
        add(i, part, sibr.at[i])

    last = nz - 1
    two_cores(2)
    pl.semaphore_wait(known.at[0], len(line_x))
    for dev in line_z:
        signal(known.at[1], dev)
    up = pass_on(2, low, rsr.at[0, low], 0, 1)
    down = pass_on(2, high, rsr.at[0, high], 1, last)
    two_cores(1)
    up_direct = pass_on(1, high, rsr.at[1, high], 2, 1)
    two_cores(last)
    down_direct = pass_on(last, low, rsr.at[2, low], 3, last)
    up.wait_recv()
    add(1, 0, rsr.at[0])
    up_sum = pass_on(1, low, rsr.at[1, low], 4, 1)
    down.wait_recv()
    add(last, part, rsr.at[0])
    down_sum = pass_on(last, high, rsr.at[2, high], 5, last)
    rs_copies = [up, down, up_direct, down_direct, up_sum, down_sum]
    mine_copies[0].wait()
    sib_copies[0].wait_recv()

    load_first = local(first_hbm, first, load_sem.at[0])
    load_second = local(second_hbm, second, load_sem.at[1])
    load_left = local(left_hbm, new_left, load_sem.at[2])
    load_right = local(right_hbm, new_right, load_sem.at[3])

    def left_part(h):
        at = shares[h]
        band = left.at[z, c, at]
        copies = [
            send(
                lb.at[plus(i), at], band, l_ss.at[h, i], l_rs.at[h, i], peer(dp, plus(i))
            )
            for i in range(1, nz)
        ]
        return copies, local(lb.at[z, at], band, l_rs.at[h, 0])

    def left_sibling(h, copies, own):
        own.wait()
        for copy in copies:
            copy.wait_recv()
        bands = left.at[:, c, shares[h]]
        return send(bands, bands, l_sib_ss.at[h], l_sib_rs.at[h], sibling)

    l_copies, l_own = left_part(0)

    for copy in rs_copies[2:]:
        copy.wait_recv()

    @pl.loop(0, blocks // step)
    def _(b):
        at = pl.ds(b * step, step)
        total = mine[0, at].astype(f32) + sibr[0, at].astype(f32)
        total = total + rsr[1, at].astype(f32) + rsr[2, at].astype(f32)
        summed[at] = total.astype(bf16)

    summed[blocks] = jnp.zeros((rows, width), bf16)

    band = grad.at[c, aligned(dp, rows), aligned(z, width)]
    pl.semaphore_wait(known.at[1], len(line_z))

    def slot_rows(i):
        o, k = partner(i)
        stage[i] = summed[inv_ref[o * nz + k]]
        return o, k

    slot_rows(0)
    local(stage.at[0], band, a_rs.at[0])

    @pl.loop(1, devices)
    def _(i):
        o, k = slot_rows(i)
        send(stage.at[i], band, a_ss.at[0], a_rs.at[i // (ny * nz)], peer(o, k))

    r_own.wait()
    for copy in r_copies:
        copy.wait_recv()
    r_sib = send(right.at[c], right.at[c], one_ss.at[0], one_rs.at[0], sibling)
    l_sib = [left_sibling(0, l_copies, l_own)]

    def rotate(r):
        at = aligned(lax.rem(x + CHUNKS - r, CHUNKS), size)
        g_sib[r].wait_recv()
        total = None
        for p in range(2):
            rhs = jnp.concatenate(
                [right[c, pl.ds((2 * j + p) * width, width), :] for j in range(nz)], axis=0
            )
            term = dot(grad[p, at], rhs, ((1,), (0,)))
            total = term if total is None else total + term
        rot[at] = total.astype(bf16)

    g_sib = []
    for r in range(CHUNKS):
        piece = grad.at[c, aligned(lax.rem(x + CHUNKS - r, CHUNKS), size)]
        pltpu.make_async_copy(piece, piece, a_rs.at[r]).wait()
        g_sib.append(send(piece, piece, g_sib_ss.at[r], g_sib_rs.at[r], sibling))
        if r:
            rotate(r - 1)
    l_copies_more, l_own = left_part(1)
    rotate(CHUNKS - 1)

    def eigen(r):
        at = aligned(r, band_size)
        lhs = left[:, :, at, :].reshape(size, order)
        out = dot(lhs, rot[...], ((1,), (0,))).astype(bf16)
        eig[:, at, :] = out.reshape(2 * nz, band_size, nz * width)
        for i in range(1, nz):
            send(
                eig.at[:, at, aligned(plus(i), width)],
                ein.at[z, :, at],
                e_ss.at[i, r],
                e_rs.at[i, r],
                peer(dp, plus(i)),
            )
        local(eig.at[:, at, aligned(z, width)], ein.at[z, :, at], e_rs.at[0, r])

    l_sib[0].wait_recv()
    pl.loop(0, 3)(eigen)
    l_sib.append(left_sibling(1, l_copies_more, l_own))
    l_sib[1].wait_recv()
    pl.loop(3, CHUNKS)(eigen)

    @pl.loop(0, CHUNKS)
    def _(r):
        at = aligned(r, size)
        out = None
        for p in range(2):
            lhs = jnp.concatenate(
                [grad[p, aligned(2 * j + c, width), :] for j in range(nz)], axis=0
            )
            term = dot(lhs, grad[p, at], ((1,), (1,)))
            out = term if out is None else out + term
        out = out.astype(bf16)
        for j in range(nz):
            ggo[j, :, at] = out[j * width : (j + 1) * width]

    pair = nz // 2

    @pl.loop(0, 4)
    def _(r):
        p, h = r // 2, r % 2
        rhs = grad[p, :, aligned(h, pair * width)]
        out = dot(grad[c], rhs, ((0,), (0,))).astype(bf16)
        for j in range(nz):
            for n in range(pair):
                at = aligned(2 * (pair * h + n) + p, width)
                gto[j, :, at] = out[j * width : (j + 1) * width, n * width : (n + 1) * width]

    load_first.wait()
    load_second.wait()

    @pl.loop(0, CHUNKS)
    def _(r):
        at = aligned(r, band_size)
        for i in list(range(1, nz)) + [0]:
            k = minus(i)
            piece = ein.at[k, :, at]
            pltpu.make_async_copy(piece, piece, e_rs.at[i, r]).wait()
            e = ein[k, :, at].astype(f32)
            new_first = first_beta * first[k, :, at] + (1.0 - first_beta) * e
            new_second = second_beta * second[k, :, at] + (1.0 - second_beta) * e * e
            first[k, :, at] = new_first
            second[k, :, at] = new_second
            nout[k, :, at] = (new_first / (jnp.sqrt(new_second) + epsilon)).astype(bf16)
            if i:
                send(
                    nout.at[k, :, at],
                    normed.at[:, at, aligned(z, width)],
                    n_ss.at[i, r],
                    n_rs.at[i, r],
                    peer(dp, k),
                )
            else:
                local(nout.at[k, :, at], normed.at[:, at, aligned(z, width)], n_rs.at[0, r])

    def outer_send(out, into, ss, rs):
        copies = [
            send(out.at[plus(i)], into.at[z], ss.at[i], rs.at[i], peer(dp, plus(i)))
            for i in range(1, nz)
        ]
        return copies, local(out.at[z], into.at[z], rs.at[0])

    gg_copies, gg_own = outer_send(ggo, ggt_in, gg_ss, gg_rs)

    for i in range(nz):
        for r in range(CHUNKS):
            piece = normed.at[:, pl.ds(r * band_size, band_size), aligned(plus(i), width)]
            pltpu.make_async_copy(piece, piece, n_rs.at[i, r]).wait()

    r_sib.wait_recv()

    @pl.loop(0, CHUNKS)
    def _(r):
        at = aligned(r, size)
        lhs = left[:, :, :, at].reshape(order, size)
        rhs = normed[...].reshape(order, nz * width)
        back[c, at] = dot(lhs, rhs, ((0,), (0,))).astype(bf16)
        send(back.at[c, at], back.at[c, at], b_sib_ss.at[r], b_sib_rs.at[r], sibling)

    for r in range(CHUNKS):
        piece = back.at[1 - c, pl.ds(r * size, size)]
        pltpu.make_async_copy(piece, piece, b_sib_rs.at[r]).wait()

    per_chunk = n_dp // CHUNKS
    my_slot = dp * nz + z

    @pl.loop(0, CHUNKS)
    def _(r):
        rr = lax.rem(r + dp // per_chunk, CHUNKS)
        at = aligned(rr, size)
        total = None
        for p in range(2):
            rhs = jnp.concatenate(
                [right[p, aligned(2 * j + c, width), :] for j in range(nz)], axis=0
            )
            term = dot(back[p, at], rhs, ((1,), (1,)))
            total = term if total is None else total + term
        ucols[at] = total.astype(bf16)

        @pl.loop(0, per_chunk * nz)
        def _(q):
            dd = rr * per_chunk + lax.rem(dp + q // nz, per_chunk)
            j = lax.rem(z + q % nz, nz)
            src = ucols.at[aligned(dd, rows), aligned(j, width)]
            own = jnp.logical_and(dd == dp, j == z)

            @pl.when(own)
            def _():
                local(src, uin.at[my_slot], a_rs.at[CHUNKS])

            @pl.when(jnp.logical_not(own))
            def _():
                send(src, uin.at[my_slot], a_ss.at[1], a_rs.at[CHUNKS], peer(dd, j))

    gt_copies, gt_own = outer_send(gto, gtg_in, gt_ss, gt_rs)

    def factors(load, into, outer, own, copies):
        load.wait()
        for i in range(nz):
            k = minus(i)
            (copies[i - 1].wait_recv if i else own.wait)()

            @pl.loop(0, width // 32)
            def _(b):
                at = pl.ds(b * 32, 32)
                into[k, at] = second_beta * into[k, at] + (1.0 - second_beta) * outer[
                    k, at
                ].astype(f32)

    factors(load_left, new_left, ggt_in, gg_own, gg_copies)
    pltpu.make_async_copy(uin, uin, a_rs.at[CHUNKS]).wait()

    @pl.loop(0, blocks)
    def _(b):
        upd[b] = uin[slot_ref[b]]

    factors(load_right, new_right, gtg_in, gt_own, gt_copies)

    for copies in (r_copies, l_copies, l_copies_more, rs_copies, l_sib, g_sib, [r_sib], gg_copies, gt_copies):
        for copy in copies:
            copy.wait_send()
    for i in turns:
        sib_copies[i].wait_send()
    sent = stage.at[pl.ds(0, devices - 1)]
    for n in range(2):
        pltpu.make_async_copy(sent, sent, a_ss.at[n]).wait()

    @pl.loop(0, CHUNKS)
    def _(r):
        at, band = aligned(r, size), aligned(r, band_size)
        for i in range(1, nz):
            piece = eig.at[:, band, aligned(plus(i), width)]
            pltpu.make_async_copy(piece, piece, e_ss.at[i, r]).wait()
            piece = nout.at[minus(i), :, band]
            pltpu.make_async_copy(piece, piece, n_ss.at[i, r]).wait()
        piece = back.at[c, at]
        pltpu.make_async_copy(piece, piece, b_sib_ss.at[r]).wait()


def write_out(*refs):
    count = len(refs) // 2
    sems = refs[-1]
    copies = []
    for n in range(count):
        for k in range(sems.shape[1]):
            share = refs[n].shape[0] // sems.shape[1]
            at = pl.ds(k * share, share)
            copy = pltpu.make_async_copy(refs[n].at[at], refs[count + n].at[at], sems.at[n, k])
            copy.start()
            copies.append(copy)
    for copy in copies:
        copy.wait()


def by_band(array):
    slots, order, width = array.shape
    return array.reshape(slots, order // width, width, width)


def run_step(
    slot_of_block, partial, left_basis, right_basis, left_factor, right_factor, first, second
):
    blocks, rows, order = partial.shape
    nz, width = left_basis.shape[0], left_basis.shape[1]
    n_dp = lax.axis_size("dp")
    slots = n_dp * nz
    half = nz * width
    operands = (slot_of_block, partial, left_basis, right_basis)
    operands += (left_factor, right_factor, by_band(first), by_band(second))
    operands = [pltpu.with_memory_space_constraint(array, pltpu.HBM) for array in operands]
    vmem = pl.BlockSpec(memory_space=pltpu.VMEM)
    hbm = pl.BlockSpec(memory_space=pltpu.HBM)
    dma = pltpu.SemaphoreType.DMA
    scratch = [
        pltpu.SMEM(slot_of_block.shape, jnp.int32),
        pltpu.SMEM((slots,), jnp.int32),
        pltpu.VMEM((nz, 2 * nz, width, width), bf16),
        pltpu.VMEM((nz, width, order), bf16),
        pltpu.VMEM((nz, width, order), bf16),
        pltpu.VMEM((nz, blocks, rows, width), bf16),
        pltpu.VMEM((nz, blocks, rows, width), bf16),
        pltpu.VMEM((3, blocks, rows, width), bf16),
        pltpu.VMEM((blocks + 1, rows, width), bf16),
        pltpu.VMEM((slots, rows, width), bf16),
        pltpu.VMEM((2, order, half), bf16),
        pltpu.VMEM((nz, 2, width, order), bf16),
        pltpu.VMEM((2, order, half), bf16),
        pltpu.VMEM((order, half), bf16),
        pltpu.VMEM((2 * nz, width, half), bf16),
        pltpu.VMEM((nz, 2 * nz, width, width), bf16),
        pltpu.VMEM((2 * nz, width, half), bf16),
        pltpu.VMEM((2, order, half), bf16),
        pltpu.VMEM((nz, width, order), bf16),
        pltpu.VMEM((nz, width, order), bf16),
        pltpu.VMEM((order, half), bf16),
        pltpu.VMEM((slots, rows, width), bf16),
        dma((5,)),
        dma((nz,)),
        dma((nz,)),
        dma((nz,)),
        dma((6,)),
        dma((6,)),
        dma((2,)),
        dma((CHUNKS + 1,)),
        dma((nz,)),
        dma((nz,)),
        dma((2, nz)),
        dma((2, nz)),
        dma((nz,)),
        dma((nz,)),
        dma((nz,)),
        dma((nz,)),
        dma((nz, CHUNKS)),
        dma((nz, CHUNKS)),
        dma((nz, CHUNKS)),
        dma((nz, CHUNKS)),
        dma((CHUNKS,)),
        dma((CHUNKS,)),
        dma((2,)),
        dma((2,)),
        dma((CHUNKS,)),
        dma((CHUNKS,)),
        dma((1,)),
        dma((1,)),
        pltpu.SemaphoreType.REGULAR((2,)),
    ]
    results = pl.pallas_call(
        functools.partial(step_kernel, n_dp, nz),
        out_shape=(
            jax.ShapeDtypeStruct((blocks, rows, width), bf16),
            jax.ShapeDtypeStruct((nz, width, order), f32),
            jax.ShapeDtypeStruct((nz, width, order), f32),
            jax.ShapeDtypeStruct((nz, 2 * nz, width, width), f32),
            jax.ShapeDtypeStruct((nz, 2 * nz, width, width), f32),
        ),
        in_specs=[hbm] * 8,
        out_specs=(vmem,) * 5,
        scratch_shapes=scratch,
        compiler_params=pltpu.CompilerParams(
            collective_id=0, has_side_effects=True, vmem_limit_bytes=40 * 2**20
        ),
        cost_estimate=pl.CostEstimate(
            flops=12 * order * order * half, bytes_accessed=16 * 2**20, transcendentals=0
        ),
        name="soap_step",
    )(*operands)
    update, new_left, new_right, new_first, new_second = pl.pallas_call(
        write_out,
        out_shape=[jax.ShapeDtypeStruct(array.shape, array.dtype) for array in results],
        in_specs=[pl.BlockSpec(memory_space=pl.ANY)] * 5,
        out_specs=[hbm] * 5,
        scratch_shapes=[dma((5, 4))],
        compiler_params=pltpu.CompilerParams(vmem_limit_bytes=2**20),
        name="write_out",
    )(*results)
    return update, new_left, new_right, new_first.reshape(first.shape), new_second.reshape(first.shape)


def per_device(
    grad_partial,
    slot_of_block,
    left_factor,
    right_factor,
    left_basis,
    right_basis,
    first_moment,
    second_moment,
):
    return run_step(
        slot_of_block,
        grad_partial[0],
        left_basis,
        right_basis,
        left_factor,
        right_factor,
        first_moment,
        second_moment,
    )


def solution(mesh):
    in_specs = (
        P("tensor", None, "dp", None),
        P(),
        P("dp", "tensor", None),
        P("dp", "tensor", None),
        P("dp", "tensor", None),
        P("dp", None, "tensor"),
        P("dp", None, "tensor"),
        P("dp", None, "tensor"),
    )
    out_specs = (
        P(None, "dp", "tensor"),
        P("dp", "tensor", None),
        P("dp", "tensor", None),
        P("dp", None, "tensor"),
        P("dp", None, "tensor"),
    )
    return jax.shard_map(
        per_device, mesh=mesh, in_specs=in_specs, out_specs=out_specs, check_vma=False
    )
```
